512 devices in a mesh: row: 32 (over z_lo, x), col: 16 (over y, z_hi, core).
Axes of the slice: x: 4, y: 4, z: 16 (z_hi: 2, z_lo: 8; z = z_hi * 8 + z_lo), core: 2. Of those that a mesh axis runs over, the one named last changes fastest.
Arguments:
- iterate: float32 [3584, 9216], P('row', 'col'), may hold values from -0.09375 to 0.09375
Outputs:
- update: float32 [3584, 9216], P('row', 'col')
The draws below stay inside these ranges and needn't reach their ends.
All inputs are finite; a program needn't handle non-finite values.
Results may differ from the reference program's by a relative error of at most 0.000068.
Values sent between devices are 32-bit elements; how exact they have to be, the bound alone decides.
No kernel may reach another device: no remote copies, remote signals or barrier semaphores. Data moves between devices by JAX's collectives and lax.ppermute only.
A program may use at most 64 MiB of HBM per device.

```python
import math
import jax
import jax.numpy as jnp
from jax import lax

M = 3584
N = 9216


def draw_iterate(key, part):
    key = jax.random.fold_in(key, 11)
    key_noise, key_rows, key_cols = jax.random.split(key, 3)
    noise = jax.random.truncated_normal(key_noise, -6.0, 6.0, (M, N), jnp.float32)
    row_scale = jnp.exp(jax.random.uniform(key_rows, (M, 1), jnp.float32) * math.log(10.0))
    col_scale = jnp.exp(jax.random.uniform(key_cols, (1, N), jnp.float32) * math.log(10.0))
    factor = 0.3 / (21.0 * math.sqrt(N))
    return noise * row_scale * col_scale * factor


def setup_inputs(seed: int = 0) -> dict:
    splits = jax.random.split(jax.random.key(seed), 2)
    iterate = draw_iterate(jax.random.fold_in(splits[1], 71), 0)
    return {"iterate": iterate}


HIGHEST_PREC = lax.Precision.HIGHEST
COEF_A = 3.4445
COEF_B = -4.775
COEF_C = 2.0315

def reference(iterate):
    gram = jnp.dot(iterate, iterate.T, precision=HIGHEST_PREC, preferred_element_type=jnp.float32)
    gram_sq = jnp.dot(gram, gram, precision=HIGHEST_PREC, preferred_element_type=jnp.float32)
    poly = COEF_B * gram + COEF_C * gram_sq
    applied = jnp.dot(poly, iterate, precision=HIGHEST_PREC, preferred_element_type=jnp.float32)
    return (COEF_A * iterate + applied) * (0.2 * math.sqrt(max(M, N)))
```

```python
import math

import jax
import jax.numpy as jnp
from jax import lax
from jax.sharding import PartitionSpec as P

M = 3584
N = 9216

HIGHEST_PREC = lax.Precision.HIGHEST
COEF_A = 3.4445
COEF_B = -4.775
COEF_C = 2.0315
AXES = ("row", "col")

X_GROUPS = [[zl * 4 + x for x in range(4)] for zl in range(8)]
ZLO_GROUPS = [[zl * 4 + x for zl in range(8)] for x in range(4)]
Y_GROUPS = [[y * 4 + k for y in range(4)] for k in range(4)]
CORE_GROUPS = [[p * 2, p * 2 + 1] for p in range(8)]


def device(x, y, z, core):
    return ((z % 8) * 4 + x) * 16 + y * 4 + (z // 8) * 2 + core


CHIPS = [(x, y, z) for x in range(4) for y in range(4) for z in range(16)]
FAR_GROUPS = [
    [device(x, y, (a * 4 + b), c) for a in range(4)]
    for x in range(4) for y in range(4) for b in range(4) for c in range(2)
]


def permute(value, target):
    pairs = [
        (device(x, y, z, c), device(*target(x, y, z, c))) for x, y, z in CHIPS for c in range(2)
    ]
    return lax.ppermute(value, AXES, pairs)


def z_shift(value, step):
    return permute(value, lambda x, y, z, c: (x, y, (z + step) % 16, c))


def dot(left, right, dims):
    return lax.dot_general(
        left, right, (dims, ((), ())), precision=HIGHEST_PREC, preferred_element_type=jnp.float32
    )


def rows_at(value, start, size):
    return lax.dynamic_slice_in_dim(value, start, size, 0)


def body(iterate):
    rows, cols = iterate.shape
    part = cols // 8
    row, col = lax.axis_index("row"), lax.axis_index("col")
    core = col % 2
    z = (col // 2 % 2) * 8 + row // 4

    with jax.named_scope("to_planes"):
        blocks = iterate.T.reshape(8, part, rows)
        blocks = lax.all_to_all(blocks, "row", 0, 0, axis_index_groups=ZLO_GROUPS)
        own = blocks.transpose(1, 0, 2).reshape(part, 8 * rows)
    with jax.named_scope("faces"):
        across = permute(own, lambda x, y, z, c: (y, x, z, c))
        left = lax.all_gather(own, "col", axis=0, tiled=True, axis_index_groups=Y_GROUPS)
        right = lax.all_gather(across, "row", axis=0, tiled=True, axis_index_groups=X_GROUPS)
    size = left.shape[1]
    half, chunk = size // 2, size // 8

    with jax.named_scope("gram"):
        partial = dot(left, right, ((0,), (0,)))
        other = rows_at(partial, (1 - core) * half, half)
        mine = rows_at(partial, core * half, half)
        total = mine + permute(other, lambda x, y, z, c: (x, y, z, 1 - c))
    with jax.named_scope("reduce_near"):
        here = rows_at(total, z % 4 * chunk, chunk)
        up = z_shift(rows_at(total, (z + 1) % 4 * chunk, chunk), 1)
        down = z_shift(rows_at(total, (z + 3) % 4 * chunk, chunk), -1)
        start = (z + 2) % 4 * chunk
        up_two = z_shift(rows_at(total, start, chunk // 2), 2)
        down_two = z_shift(rows_at(total, start + chunk // 2, chunk // 2), -2)
        near = here + up + down + jnp.concatenate([up_two, down_two], 0)
    with jax.named_scope("reduce_far"):
        pieces = near.reshape(4, chunk // 4, size)
        pieces = lax.all_to_all(pieces, AXES, 0, 0, axis_index_groups=FAR_GROUPS)
        piece = jnp.sum(pieces, 0)
    with jax.named_scope("gather_far"):
        pieces = jnp.broadcast_to(piece, (4,) + piece.shape)
        pieces = lax.all_to_all(pieces, AXES, 0, 0, axis_index_groups=FAR_GROUPS)
        near = pieces.reshape(chunk, size)
    with jax.named_scope("gather_near"):
        from_below = z_shift(near, 1)
        from_above = z_shift(near, -1)
        first = z_shift(near[: chunk // 2], -2)
        second = z_shift(near[chunk // 2 :], 2)
        total = jnp.zeros((half, size), jnp.float32)
        put = lax.dynamic_update_slice_in_dim
        total = put(total, near, z % 4 * chunk, 0)
        total = put(total, from_below, (z + 3) % 4 * chunk, 0)
        total = put(total, from_above, (z + 1) % 4 * chunk, 0)
        total = put(total, first, start, 0)
        total = put(total, second, start + chunk // 2, 0)
    with jax.named_scope("gather_core"):
        gram = lax.all_gather(total, "col", axis=0, tiled=True, axis_index_groups=CORE_GROUPS)

    with jax.named_scope("first_product"):
        product = dot(left, gram, ((1,), (0,)))
        parts = product.reshape(4, part, size)
        parts = lax.all_to_all(parts, "row", 0, 0, axis_index_groups=X_GROUPS)
        inner = COEF_B * across + COEF_C * jnp.sum(parts, 0)
        inner = lax.all_gather(inner, "row", axis=0, tiled=True, axis_index_groups=X_GROUPS)
    with jax.named_scope("second_product"):
        product = dot(inner, gram, ((1,), (1,)))
        parts = product.reshape(4, part, size)
        parts = lax.all_to_all(parts, "col", 0, 0, axis_index_groups=Y_GROUPS)
        applied = jnp.sum(parts, 0)
    with jax.named_scope("to_blocks"):
        blocks = applied.reshape(part, 8, rows).transpose(1, 0, 2)
        blocks = lax.all_to_all(blocks, "row", 0, 0, axis_index_groups=ZLO_GROUPS)
        applied = blocks.reshape(cols, rows).T
    return (COEF_A * iterate + applied) * (0.2 * math.sqrt(max(M, N)))


def solution(mesh):
    placed = (P("row", "col"),)
    return jax.shard_map(
        body, mesh=mesh, in_specs=placed, out_specs=P("row", "col"), check_vma=False
    )
```

```python
import math

import jax
import jax.numpy as jnp
from jax import lax
from jax.sharding import PartitionSpec as P

M = 3584
N = 9216

PREC = lax.Precision.HIGHEST
COEF_A = 3.4445
COEF_B = -4.775
COEF_C = 2.0315
AXES = ("row", "col")

X_GROUPS = [[zl * 4 + x for x in range(4)] for zl in range(8)]
B_GROUPS = [[(q * 4 + b) * 4 + x for b in range(4)] for q in range(2) for x in range(4)]
Y_GROUPS = [[y * 4 + k for y in range(4)] for k in range(4)]


def device(x, y, z, core):
    return ((z % 8) * 4 + x) * 16 + y * 4 + (z // 8) * 2 + core


CHIPS = [(x, y, z) for x in range(4) for y in range(4) for z in range(16)]
A_GROUPS = [
    [device(x, y, (a * 4 + b), c) for a in range(4)]
    for x in range(4) for y in range(4) for b in range(4) for c in range(2)
]


def permute(value, target):
    pairs = [
        (device(x, y, z, c), device(*target(x, y, z, c))) for x, y, z in CHIPS for c in range(2)
    ]
    return lax.ppermute(value, AXES, pairs)


def swap_q(value):
    return permute(value, lambda x, y, z, c: (x, y, z ^ 4, c))


def swap_core(value):
    return permute(value, lambda x, y, z, c: (x, y, z, 1 - c))


def b_shift(value, step):
    return permute(value, lambda x, y, z, c: (x, y, z // 4 * 4 + (z + step) % 4, c))


def dot(left, right, dims):
    return lax.dot_general(
        left, right, (dims, ((), ())), precision=PREC, preferred_element_type=jnp.float32
    )


def rows_at(value, start, size):
    return lax.dynamic_slice_in_dim(value, start, size, 0)


def ordered(index, own, other):
    return jnp.where(index == 0, own, other), jnp.where(index == 0, other, own)


def body(iterate):
    rows, cols = iterate.shape
    depth = cols // 2
    row, col = lax.axis_index("row"), lax.axis_index("col")
    core = col % 2
    x, b, q = row % 4, row // 4 % 4, row // 16

    with jax.named_scope("swap_columns"):
        flipped = iterate.T
        own = rows_at(flipped, q * depth, depth)
        other = swap_q(rows_at(flipped, (1 - q) * depth, depth))
        block = jnp.concatenate(ordered(q, own, other), 1)
    with jax.named_scope("faces"):
        shifted = [block] + [b_shift(block, s) for s in (1, 2, 3)]
        right = lax.all_gather(block, "row", axis=0, axis_index_groups=X_GROUPS)
        right = right.transpose(1, 0, 2).reshape(depth, 8 * rows)
        left = jnp.zeros((4,) + block.shape, jnp.float32)
        for s in range(4):
            left = lax.dynamic_update_slice_in_dim(left, shifted[s][None], (b + 4 - s) % 4, 0)
        left = left.transpose(1, 0, 2).reshape(depth, 8 * rows)
    size = 8 * rows
    half, chunk = size // 2, size // 8

    with jax.named_scope("gram"):
        partial = dot(left, right, ((0,), (0,)))
        total = rows_at(partial, core * half, half) + swap_core(
            rows_at(partial, (1 - core) * half, half)
        )
    with jax.named_scope("reduce_y"):
        parts = lax.all_to_all(
            total.reshape(4, chunk, size), "col", 0, 0, axis_index_groups=Y_GROUPS
        )
        near = jnp.sum(parts, 0)
    with jax.named_scope("reduce_a"):
        parts = near.reshape(4, chunk // 4, size)
        parts = lax.all_to_all(parts, AXES, 0, 0, axis_index_groups=A_GROUPS)
        piece = jnp.sum(parts, 0)
    with jax.named_scope("gather_a"):
        parts = jnp.broadcast_to(piece, (4,) + piece.shape)
        parts = lax.all_to_all(parts, AXES, 0, 0, axis_index_groups=A_GROUPS)
        near = parts.reshape(chunk, size)
    with jax.named_scope("gather_y"):
        parts = jnp.broadcast_to(near, (4,) + near.shape)
        parts = lax.all_to_all(parts, "col", 0, 0, axis_index_groups=Y_GROUPS)
        total = parts.reshape(half, size)
    with jax.named_scope("gather_core"):
        gram = jnp.concatenate(ordered(core, total, swap_core(total)), 0)

    with jax.named_scope("first_product"):
        product = dot(left, gram, ((1,), (0,)))
        parts = product.reshape(4, depth // 4, size)
        parts = lax.all_to_all(parts, "row", 0, 0, axis_index_groups=X_GROUPS)
        mine = rows_at(right, x * (depth // 4), depth // 4)
        inner = COEF_B * mine + COEF_C * jnp.sum(parts, 0)
        inner = lax.all_gather(inner, "row", axis=0, tiled=True, axis_index_groups=X_GROUPS)
    with jax.named_scope("second_product"):
        product = dot(inner, gram, ((1,), (1,)))
        parts = product.reshape(depth, 4, 2 * rows).transpose(1, 0, 2)
        parts = lax.all_to_all(parts, "row", 0, 0, axis_index_groups=B_GROUPS)
        applied = jnp.sum(parts, 0)
    with jax.named_scope("swap_back"):
        first, second = applied[:, :rows], applied[:, rows:]
        own, other = ordered(q, first, second)
        applied = jnp.concatenate(ordered(q, own, swap_q(other)), 0).T
    return (COEF_A * iterate + applied) * (0.2 * math.sqrt(max(M, N)))


def solution(mesh):
    placed = (P("row", "col"),)
    return jax.shard_map(
        body, mesh=mesh, in_specs=placed, out_specs=P("row", "col"), check_vma=False
    )
```

```python
import math

import jax
import jax.numpy as jnp
from jax import lax
from jax.experimental.layout import Layout, with_layout_constraint
from jax.sharding import PartitionSpec as P

M = 3584
N = 9216

PREC = lax.Precision.HIGHEST
COEF_A = 3.4445
COEF_B = -4.775
COEF_C = 2.0315
AXES = ("row", "col")

X_GROUPS = [[zl * 4 + x for x in range(4)] for zl in range(8)]
Y_GROUPS = [[y * 4 + k for y in range(4)] for k in range(4)]


def device(x, y, z, core):
    return ((z % 8) * 4 + x) * 16 + y * 4 + (z // 8) * 2 + core


CHIPS = [(x, y, z) for x in range(4) for y in range(4) for z in range(16)]
A_GROUPS = [
    [device(x, y, (a * 4 + b), c) for a in range(4)]
    for x in range(4) for y in range(4) for b in range(4) for c in range(2)
]


def permute(value, target):
    pairs = [
        (device(x, y, z, c), device(*target(x, y, z, c))) for x, y, z in CHIPS for c in range(2)
    ]
    return lax.ppermute(value, AXES, pairs)


def swap_q(value):
    return permute(value, lambda x, y, z, c: (x, y, z ^ 4, c))


def swap_core(value):
    return permute(value, lambda x, y, z, c: (x, y, z, 1 - c))


def b_shift(value, step):
    return permute(value, lambda x, y, z, c: (x, y, z // 4 * 4 + (z + step) % 4, c))


def dot(left, right, dims):
    return lax.dot_general(
        left, right, (dims, ((), ())), precision=PREC, preferred_element_type=jnp.float32
    )


def rows_at(value, start, size):
    return lax.dynamic_slice_in_dim(value, start, size, 0)


def in_rows(value):
    return with_layout_constraint(value, Layout(major_to_minor=(0, 1)))


def ordered(index, own, other):
    return jnp.where(index == 0, own, other), jnp.where(index == 0, other, own)


def body(iterate):
    rows, cols = iterate.shape
    depth = cols // 2
    row, col = lax.axis_index("row"), lax.axis_index("col")
    core = col % 2
    x, q = row % 4, row // 16

    with jax.named_scope("swap_columns"):
        flipped = in_rows(iterate.T)
        own = in_rows(rows_at(flipped, q * depth, depth))
        other = in_rows(swap_q(in_rows(rows_at(flipped, (1 - q) * depth, depth))))
    with jax.named_scope("faces"):
        lefts = []
        for s in range(4):
            parts = (own, other) if s == 0 else (b_shift(own, s), b_shift(other, s))
            lefts.append(jnp.concatenate(ordered(q, *parts), 1))
        near = jnp.concatenate(lefts[:2], 1)
        far = jnp.concatenate(lefts[2:], 1)
        kept, given = ordered(core, near, far)
        right = [
            lax.all_gather(part, "row", axis=0, axis_index_groups=X_GROUPS)
            for part in (own, other)
        ]
        right = jnp.concatenate(ordered(q, *right), 0)
        right = right.transpose(1, 0, 2).reshape(depth, 8 * rows)
    size = 8 * rows
    half, chunk = size // 2, size // 8

    with jax.named_scope("gram"):
        partial = swap_core(dot(given, right, ((0,), (0,))))
        total = dot(kept, right, ((0,), (0,))) + partial
    with jax.named_scope("reduce_y"):
        parts = lax.all_to_all(
            total.reshape(4, chunk, size), "col", 0, 0, axis_index_groups=Y_GROUPS
        )
        near = jnp.sum(parts, 0)
    with jax.named_scope("reduce_a"):
        parts = near.reshape(4, chunk // 4, size)
        parts = lax.all_to_all(parts, AXES, 0, 0, axis_index_groups=A_GROUPS)
        piece = jnp.sum(parts, 0)
    with jax.named_scope("gather_a"):
        parts = jnp.broadcast_to(piece, (4,) + piece.shape)
        parts = lax.all_to_all(parts, AXES, 0, 0, axis_index_groups=A_GROUPS)
        near = parts.reshape(chunk, size)
    with jax.named_scope("gather_y"):
        parts = jnp.broadcast_to(near, (4,) + near.shape)
        parts = lax.all_to_all(parts, "col", 0, 0, axis_index_groups=Y_GROUPS)
        gram_kept = parts.reshape(half, size)
    with jax.named_scope("gather_core"):
        gram_given = swap_core(gram_kept)

    with jax.named_scope("first_product"):
        product = dot(kept, gram_kept, ((1,), (0,))) + dot(given, gram_given, ((1,), (0,)))
        parts = product.reshape(4, depth // 4, size)
        parts = lax.all_to_all(parts, "row", 0, 0, axis_index_groups=X_GROUPS)
        mine = rows_at(right, x * (depth // 4), depth // 4)
        inner = COEF_B * mine + COEF_C * jnp.sum(parts, 0)
        inner = lax.all_gather(inner, "row", axis=0, tiled=True, axis_index_groups=X_GROUPS)
    with jax.named_scope("second_product"):
        near, far = ordered(
            core,
            in_rows(dot(inner, gram_kept, ((1,), (1,)))),
            in_rows(dot(inner, gram_given, ((1,), (1,)))),
        )
        sums = []
        for part in (1 - q, q):
            blocks = []
            for s in range(4):
                value = (near, far)[s // 2][:, s % 2 * 2 * rows :][:, : 2 * rows]
                block = in_rows(jnp.where(part == 0, value[:, :rows], value[:, rows:]))
                blocks.append(b_shift(block, -s) if s else block)
            sums.append(blocks[0] + blocks[1] + blocks[2] + blocks[3])
    with jax.named_scope("swap_back"):
        applied = jnp.concatenate(ordered(q, sums[1], swap_q(sums[0])), 0).T
    return (COEF_A * iterate + applied) * (0.2 * math.sqrt(max(M, N)))


def solution(mesh):
    placed = (P("row", "col"),)
    return jax.shard_map(
        body, mesh=mesh, in_specs=placed, out_specs=P("row", "col"), check_vma=False
    )
```

```python
import math

import jax
import jax.numpy as jnp
from jax import lax
from jax.experimental.layout import Layout, with_layout_constraint
from jax.sharding import PartitionSpec as P

M = 3584
N = 9216

PREC = lax.Precision.HIGHEST
COEF_A = 3.4445
COEF_B = -4.775
COEF_C = 2.0315
AXES = ("row", "col")

X_GROUPS = [[zl * 4 + x for x in range(4)] for zl in range(8)]
B_GROUPS = [[(q * 4 + b) * 4 + x for b in range(4)] for q in range(2) for x in range(4)]
Y_GROUPS = [[y * 4 + k for y in range(4)] for k in range(4)]


def device(x, y, z, core):
    return ((z % 8) * 4 + x) * 16 + y * 4 + (z // 8) * 2 + core


CHIPS = [(x, y, z) for x in range(4) for y in range(4) for z in range(16)]
A_GROUPS = [
    [device(x, y, (a * 4 + b), c) for a in range(4)]
    for x in range(4) for y in range(4) for b in range(4) for c in range(2)
]


def permute(value, target):
    pairs = [
        (device(x, y, z, c), device(*target(x, y, z, c))) for x, y, z in CHIPS for c in range(2)
    ]
    return lax.ppermute(value, AXES, pairs)


def swap_q(value):
    return permute(value, lambda x, y, z, c: (x, y, z ^ 4, c))


def swap_core(value):
    return permute(value, lambda x, y, z, c: (x, y, z, 1 - c))


def b_shift(value, step):
    return permute(value, lambda x, y, z, c: (x, y, z // 4 * 4 + (z + step) % 4, c))


def dot(left, right, dims):
    return lax.dot_general(
        left, right, (dims, ((), ())), precision=PREC, preferred_element_type=jnp.float32
    )


def rows_at(value, start, size):
    return lax.dynamic_slice_in_dim(value, start, size, 0)


def in_rows(value):
    return with_layout_constraint(value, Layout(major_to_minor=(0, 1)))


def ordered(index, own, other):
    return jnp.where(index == 0, own, other), jnp.where(index == 0, other, own)


def joined(blocks, part, rows):
    blocks = blocks.reshape(4, part, 4, 2 * rows).transpose(2, 1, 0, 3)
    return blocks.reshape(4 * part, 8 * rows)


def body(iterate):
    rows, cols = iterate.shape
    depth = cols // 2
    row, col = lax.axis_index("row"), lax.axis_index("col")
    core = col % 2
    x, b, q = row % 4, row // 4 % 4, row // 16

    with jax.named_scope("swap_columns"):
        flipped = in_rows(iterate.T)
        own = in_rows(rows_at(flipped, q * depth, depth))
        other = in_rows(swap_q(in_rows(rows_at(flipped, (1 - q) * depth, depth))))
    with jax.named_scope("faces"):
        block = jnp.concatenate(ordered(q, own, other), 1)
        part = depth // 4
        block = block.reshape(4, part, 2 * rows).transpose(1, 0, 2).reshape(part, 8 * rows)
        blocks = jnp.broadcast_to(block, (4,) + block.shape)
        right = lax.all_to_all(blocks, "row", 0, 0, axis_index_groups=X_GROUPS)
        right = joined(right, part, rows)
        left = lax.all_gather(block, "row", axis=0, axis_index_groups=B_GROUPS)
        left = rows_at(jnp.concatenate([left, left], 0), b, 4)
        left = joined(left, part, rows)
    size = 8 * rows
    half, chunk = size // 2, size // 8

    with jax.named_scope("gram"):
        kept, given = ordered(core, left[:, :half], left[:, half:])
        partial = swap_core(dot(given, right, ((0,), (0,))))
        total = lax.optimization_barrier(dot(kept, right, ((0,), (0,))))
        total = total + partial
    with jax.named_scope("reduce_y"):
        parts = lax.all_to_all(
            total.reshape(4, chunk, size), "col", 0, 0, axis_index_groups=Y_GROUPS
        )
        near = jnp.sum(parts, 0)
    with jax.named_scope("reduce_a"):
        parts = near.reshape(4, chunk // 4, size)
        parts = lax.all_to_all(parts, AXES, 0, 0, axis_index_groups=A_GROUPS)
        piece = jnp.sum(parts, 0)
    with jax.named_scope("gather_a"):
        parts = lax.all_gather(piece, AXES, axis=0, axis_index_groups=A_GROUPS)
        near = parts.reshape(chunk, size)
    with jax.named_scope("gather_y"):
        parts = jnp.broadcast_to(near, (4,) + near.shape)
        parts = lax.all_to_all(parts, "col", 0, 0, axis_index_groups=Y_GROUPS)
        gram_kept = parts.reshape(half, size)
    with jax.named_scope("gather_core"):
        gram_given = swap_core(gram_kept)

    with jax.named_scope("first_product"):
        product = lax.optimization_barrier(dot(kept, gram_kept, ((1,), (0,))))
        product = product + dot(given, gram_given, ((1,), (0,)))
        parts = product.reshape(4, depth // 4, size)
        parts = lax.all_to_all(parts, "row", 0, 0, axis_index_groups=X_GROUPS)
        mine = rows_at(right, x * (depth // 4), depth // 4)
        inner = COEF_B * mine + COEF_C * jnp.sum(parts, 0)
        inner = lax.all_gather(inner, "row", axis=0, tiled=True, axis_index_groups=X_GROUPS)
    with jax.named_scope("second_product"):
        near, far = ordered(
            core,
            in_rows(dot(inner, gram_kept, ((1,), (1,)))),
            in_rows(dot(inner, gram_given, ((1,), (1,)))),
        )
        sums = []
        for part in (1 - q, q):
            blocks = []
            for s in range(4):
                value = (near, far)[s // 2][:, s % 2 * 2 * rows :][:, : 2 * rows]
                block = in_rows(jnp.where(part == 0, value[:, :rows], value[:, rows:]))
                blocks.append(b_shift(block, s) if s else block)
            sums.append(blocks[0] + blocks[1] + blocks[2] + blocks[3])
    with jax.named_scope("swap_back"):
        applied = jnp.concatenate(ordered(q, sums[1], swap_q(sums[0])), 0).T
    return (COEF_A * iterate + applied) * (0.2 * math.sqrt(max(M, N)))


def solution(mesh):
    placed = (P("row", "col"),)
    return jax.shard_map(
        body, mesh=mesh, in_specs=placed, out_specs=P("row", "col"), check_vma=False
    )
```

```python
import math

import jax
import jax.numpy as jnp
from jax import lax
from jax.experimental.layout import Layout, with_layout_constraint
from jax.sharding import PartitionSpec as P

M = 3584
N = 9216

PREC = lax.Precision.HIGHEST
COEF_A = 3.4445
COEF_B = -4.775
COEF_C = 2.0315
AXES = ("row", "col")

X_GROUPS = [[zl * 4 + x for x in range(4)] for zl in range(8)]
B_GROUPS = [[(q * 4 + b) * 4 + x for b in range(4)] for q in range(2) for x in range(4)]
Y_GROUPS = [[y * 4 + k for y in range(4)] for k in range(4)]


def device(x, y, z, core):
    return ((z % 8) * 4 + x) * 16 + y * 4 + (z // 8) * 2 + core


CHIPS = [(x, y, z) for x in range(4) for y in range(4) for z in range(16)]
A_GROUPS = [
    [device(x, y, (a * 4 + b), c) for a in range(4)]
    for x in range(4) for y in range(4) for b in range(4) for c in range(2)
]


def permute(value, target):
    pairs = [
        (device(x, y, z, c), device(*target(x, y, z, c))) for x, y, z in CHIPS for c in range(2)
    ]
    return lax.ppermute(value, AXES, pairs)


def swap_q(value):
    return permute(value, lambda x, y, z, c: (x, y, z ^ 4, c))


def swap_core(value):
    return permute(value, lambda x, y, z, c: (x, y, z, 1 - c))


def b_shift(value, step):
    return permute(value, lambda x, y, z, c: (x, y, z // 4 * 4 + (z + step) % 4, c))


def dot(left, right, dims):
    return lax.dot_general(
        left, right, (dims, ((), ())), precision=PREC, preferred_element_type=jnp.float32
    )


def rows_at(value, start, size):
    return lax.dynamic_slice_in_dim(value, start, size, 0)


def in_rows(value):
    return with_layout_constraint(value, Layout(major_to_minor=(0, 1)))


def ordered(index, own, other):
    return jnp.where(index == 0, own, other), jnp.where(index == 0, other, own)


def joined(blocks, part, rows):
    blocks = blocks.reshape(4, part, 4, 2 * rows).transpose(2, 1, 0, 3)
    return blocks.reshape(4 * part, 8 * rows)


def tiles(value):
    rows, lanes = value.shape
    value = value.reshape(rows // 8, 8, lanes // 128, 128).transpose(0, 2, 1, 3)
    value = value.reshape(-1, 8, 128)
    each = -(-value.shape[0] // 4)
    value = jnp.pad(value, ((0, 4 * each - value.shape[0]), (0, 0), (0, 0)))
    return value.reshape(4, each, 8, 128)


def from_tiles(pieces, shape):
    rows, lanes = shape
    value = pieces.reshape(-1, 8, 128)[: rows // 8 * (lanes // 128)]
    value = value.reshape(rows // 8, lanes // 128, 8, 128).transpose(0, 2, 1, 3)
    return value.reshape(rows, lanes)


def body(iterate):
    rows, cols = iterate.shape
    depth = cols // 2
    row, col = lax.axis_index("row"), lax.axis_index("col")
    core = col % 2
    a = col // 2 % 2 * 2 + row // 16
    x, b, q = row % 4, row // 4 % 4, row // 16

    with jax.named_scope("swap_columns"):
        flipped = in_rows(iterate.T)
        own = in_rows(rows_at(flipped, q * depth, depth))
        other = in_rows(swap_q(in_rows(rows_at(flipped, (1 - q) * depth, depth))))
    with jax.named_scope("faces"):
        block = jnp.concatenate(ordered(q, own, other), 1)
        part = depth // 4
        block = block.reshape(4, part, 2 * rows).transpose(1, 0, 2).reshape(part, 8 * rows)
        blocks = jnp.broadcast_to(block, (4,) + block.shape)
        right = lax.all_to_all(blocks, "row", 0, 0, axis_index_groups=X_GROUPS)
        right = joined(right, part, rows)
        left = lax.all_gather(block, "row", axis=0, axis_index_groups=B_GROUPS)
        left = rows_at(jnp.concatenate([left, left], 0), b, 4)
        left = joined(left, part, rows)
    size = 8 * rows
    half, chunk = size // 2, size // 8

    with jax.named_scope("gram"):
        kept, given = ordered(core, left[:, :half], left[:, half:])
        partial = swap_core(dot(given, right, ((0,), (0,))))
        total = lax.optimization_barrier(dot(kept, right, ((0,), (0,))))
        total = total + partial
    with jax.named_scope("reduce_y"):
        parts = lax.all_to_all(
            total.reshape(4, chunk, size), "col", 0, 0, axis_index_groups=Y_GROUPS
        )
        near = jnp.sum(parts, 0)
    with jax.named_scope("reduce_a"):
        pieces = tiles(near)
        piece = lax.dynamic_index_in_dim(pieces, a, 0, False)
        for step in (2, 1, 3):
            sent = lax.dynamic_index_in_dim(pieces, (a + step) % 4, 0, False)
            piece = piece + permute(sent, lambda x, y, z, c: (x, y, (z + 4 * step) % 16, c))
    with jax.named_scope("gather_a"):
        pieces = lax.all_gather(piece, AXES, axis=0, axis_index_groups=A_GROUPS)
        near = from_tiles(pieces, near.shape)
    with jax.named_scope("gather_y"):
        parts = jnp.broadcast_to(near, (4,) + near.shape)
        parts = lax.all_to_all(parts, "col", 0, 0, axis_index_groups=Y_GROUPS)
        gram_kept = parts.reshape(half, size)
    with jax.named_scope("gather_core"):
        gram_given = swap_core(gram_kept)

    with jax.named_scope("first_product"):
        product = lax.optimization_barrier(dot(kept, gram_kept, ((1,), (0,))))
        product = product + dot(given, gram_given, ((1,), (0,)))
        parts = product.reshape(4, depth // 4, size)
        parts = lax.all_to_all(parts, "row", 0, 0, axis_index_groups=X_GROUPS)
        mine = rows_at(right, x * (depth // 4), depth // 4)
        inner = COEF_B * mine + COEF_C * jnp.sum(parts, 0)
        inner = lax.all_gather(inner, "row", axis=0, tiled=True, axis_index_groups=X_GROUPS)
    with jax.named_scope("second_product"):
        near, far = ordered(
            core,
            in_rows(dot(inner, gram_kept, ((1,), (1,)))),
            in_rows(dot(inner, gram_given, ((1,), (1,)))),
        )
        sums = []
        for part in (1 - q, q):
            blocks = []
            for s in range(4):
                value = (near, far)[s // 2][:, s % 2 * 2 * rows :][:, : 2 * rows]
                block = in_rows(jnp.where(part == 0, value[:, :rows], value[:, rows:]))
                blocks.append(b_shift(block, s) if s else block)
            sums.append(blocks[0] + blocks[1] + blocks[2] + blocks[3])
    with jax.named_scope("swap_back"):
        applied = jnp.concatenate(ordered(q, sums[1], swap_q(sums[0])), 0).T
    return (COEF_A * iterate + applied) * (0.2 * math.sqrt(max(M, N)))


def solution(mesh):
    placed = (P("row", "col"),)
    return jax.shard_map(
        body, mesh=mesh, in_specs=placed, out_specs=P("row", "col"), check_vma=False
    )
```

```python
import math

import jax
import jax.numpy as jnp
from jax import lax
from jax.experimental import pallas as pl
from jax.experimental.pallas import tpu as pltpu
from jax.sharding import PartitionSpec as P

M = 3584
N = 9216

PREC = lax.Precision.HIGHEST
COEF_A = 3.4445
COEF_B = -4.775
COEF_C = 2.0315
AXES = ("row", "col")

X_GROUPS = [[zl * 4 + x for x in range(4)] for zl in range(8)]
B_GROUPS = [[(q * 4 + b) * 4 + x for b in range(4)] for q in range(2) for x in range(4)]
Y_GROUPS = [[y * 4 + k for y in range(4)] for k in range(4)]


def device(x, y, z, core):
    return ((z % 8) * 4 + x) * 16 + y * 4 + (z // 8) * 2 + core


CHIPS = [(x, y, z) for x in range(4) for y in range(4) for z in range(16)]
A_GROUPS = [
    [device(x, y, (a * 4 + b), c) for a in range(4)]
    for x in range(4) for y in range(4) for b in range(4) for c in range(2)
]


def permute(value, target):
    pairs = [
        (device(x, y, z, c), device(*target(x, y, z, c))) for x, y, z in CHIPS for c in range(2)
    ]
    return lax.ppermute(value, AXES, pairs)


def swap_q(value):
    return permute(value, lambda x, y, z, c: (x, y, z ^ 4, c))


def swap_core(value):
    return permute(value, lambda x, y, z, c: (x, y, z, 1 - c))


def b_shift(value, step):
    return permute(value, lambda x, y, z, c: (x, y, z // 4 * 4 + (z + step) % 4, c))


def dot(left, right, dims):
    return lax.dot_general(
        left, right, (dims, ((), ())), precision=PREC, preferred_element_type=jnp.float32
    )


def local(kernel, shapes, index, *arrays, scratch=()):
    vmem = pl.BlockSpec(memory_space=pltpu.VMEM)
    return pl.pallas_call(
        kernel,
        out_shape=[jax.ShapeDtypeStruct(shape, jnp.float32) for shape in shapes],
        in_specs=[pl.BlockSpec(memory_space=pltpu.SMEM)] + [vmem] * len(arrays),
        out_specs=[vmem] * len(shapes),
        scratch_shapes=[pltpu.VMEM(shape, jnp.float32) for shape in scratch],
        compiler_params=pltpu.CompilerParams(vmem_limit_bytes=24 * 2**20),
    )(jnp.stack(index).astype(jnp.int32), *arrays)


ROWS, DEPTH = 112, 288
PACKED = (256, 128)


def pack(packed, value):
    packed[0:ROWS, :] = value[:, 0:128]
    packed[ROWS : 2 * ROWS, :] = value[:, 128:256]
    packed[240:256, :] = jnp.zeros((16, 128), jnp.float32)
    for g in range(4):
        n = min(32, ROWS - 32 * g)
        packed[224 : 224 + n, 32 * g : 32 * g + 32] = value[32 * g : 32 * g + n, 256:DEPTH]


def unpack(value, packed, at):
    value[0:ROWS, at : at + 128] = packed[0:ROWS, :]
    value[0:ROWS, at + 128 : at + 256] = packed[ROWS : 2 * ROWS, :]
    for g in range(4):
        n = min(32, ROWS - 32 * g)
        value[32 * g : 32 * g + n, at + 256 : at + DEPTH] = packed[
            224 : 224 + n, 32 * g : 32 * g + 32
        ]


def send_kernel(index, iterate, sent):
    for q in range(2):

        @pl.when(index[0] == q)
        def _():
            pack(sent, iterate[:, DEPTH * (1 - q) : DEPTH * (2 - q)])


def block_kernel(index, iterate, other, block, blocks, wide):
    part = DEPTH // 4

    def place(q):
        flipped = wide[...].T
        for k in range(4):
            at = k * 2 * ROWS + q * ROWS
            value = flipped[k * part : (k + 1) * part, 0:ROWS]
            block[:, at : at + ROWS] = value
            for n in range(4):
                blocks[n, :, at : at + ROWS] = value

    for q in range(2):

        @pl.when(index[0] == q)
        def _():
            wide[0:ROWS, 0:DEPTH] = iterate[:, DEPTH * q : DEPTH * (q + 1)]
            place(q)
            unpack(wide, other, 0)
            place(1 - q)


def faces_kernel(index, from_x, from_b, right, kept, given, mine):
    b, core, x = index[0], index[1], index[2]
    part, wide = DEPTH // 4, 2 * ROWS
    for n in range(4):
        for k in range(4):
            rows, lanes = pl.ds(k * part, part), pl.ds(k * wide, wide)
            right[rows, n * wide : (n + 1) * wide] = from_x[n, :, lanes]
            face = (kept, given)[n // 2]
            source = lax.rem(b + 2 * core + n, 4)
            face[rows, n % 2 * wide : (n % 2 + 1) * wide] = from_b[source, :, lanes]
    mine[...] = COEF_B * right[pl.ds(pl.multiple_of(x * part, 8), part), :]


def tail_kernel(index, kept, given, *packed):
    core, q = index[0], index[1]
    for c in range(2):

        @pl.when(core == c)
        def _():
            for s in range(4):
                source = (kept, given)[(s // 2 + c) % 2]
                for n, part in enumerate((1 - q, q)):
                    at = pl.multiple_of(s % 2 * 2 * ROWS + part * ROWS, 8)
                    pack(packed[4 * n + s], source[pl.ds(at, ROWS), :])


def final_kernel(index, iterate, own, other, update):
    for q in range(2):

        @pl.when(index[0] == q)
        def _():
            unpack(update, own, DEPTH * q)
            unpack(update, other, DEPTH * (1 - q))

    update[...] = (COEF_A * iterate[...] + update[...]) * (0.2 * math.sqrt(max(M, N)))


def tiles(value):
    rows, lanes = value.shape
    value = value.reshape(rows // 8, 8, lanes // 128, 128).transpose(0, 2, 1, 3)
    value = value.reshape(-1, 8, 128)
    each = -(-value.shape[0] // 4)
    value = jnp.pad(value, ((0, 4 * each - value.shape[0]), (0, 0), (0, 0)))
    return value.reshape(4, each, 8, 128)


def from_tiles(pieces, shape):
    rows, lanes = shape
    value = pieces.reshape(-1, 8, 128)[: rows // 8 * (lanes // 128)]
    value = value.reshape(rows // 8, lanes // 128, 8, 128).transpose(0, 2, 1, 3)
    return value.reshape(rows, lanes)


def body(iterate):
    part, size = DEPTH // 4, 8 * ROWS
    half, chunk = size // 2, size // 8
    row, col = lax.axis_index("row"), lax.axis_index("col")
    core = col % 2
    a = col // 2 % 2 * 2 + row // 16
    x, b, q = row % 4, row // 4 % 4, row // 16

    with jax.named_scope("swap_columns"):
        (sent,) = local(send_kernel, [PACKED], [q], iterate)
        other = swap_q(sent)
    with jax.named_scope("faces"):
        block, blocks = local(
            block_kernel, [(part, size), (4, part, size)], [q], iterate, other, scratch=[(128, 384)]
        )
        from_x = lax.all_to_all(blocks, "row", 0, 0, axis_index_groups=X_GROUPS)
        from_b = lax.all_gather(block, "row", axis=0, axis_index_groups=B_GROUPS)
        right, kept, given, mine = local(
            faces_kernel,
            [(DEPTH, size), (DEPTH, half), (DEPTH, half), (part, size)],
            [b, core, x],
            from_x,
            from_b,
        )

    with jax.named_scope("gram"):
        partial = swap_core(dot(given, right, ((0,), (0,))))
        total = lax.optimization_barrier(dot(kept, right, ((0,), (0,))))
        total = total + partial
    with jax.named_scope("reduce_y"):
        parts = lax.all_to_all(
            total.reshape(4, chunk, size), "col", 0, 0, axis_index_groups=Y_GROUPS
        )
        near = jnp.sum(parts, 0)
    with jax.named_scope("reduce_a"):
        pieces = tiles(near)
        piece = lax.dynamic_index_in_dim(pieces, a, 0, False)
        for step in (2, 1, 3):
            sent = lax.dynamic_index_in_dim(pieces, (a + step) % 4, 0, False)
            piece = piece + permute(sent, lambda x, y, z, c: (x, y, (z + 4 * step) % 16, c))
    with jax.named_scope("gather_a"):
        pieces = lax.all_gather(piece, AXES, axis=0, axis_index_groups=A_GROUPS)
        near = from_tiles(pieces, near.shape)
    with jax.named_scope("gather_y"):
        parts = jnp.broadcast_to(near, (4,) + near.shape)
        parts = lax.all_to_all(parts, "col", 0, 0, axis_index_groups=Y_GROUPS)
        gram_kept = parts.reshape(half, size)
    with jax.named_scope("gather_core"):
        gram_given = swap_core(gram_kept)

    with jax.named_scope("first_product"):
        product = lax.optimization_barrier(dot(kept, gram_kept, ((1,), (0,))))
        product = product + dot(given, gram_given, ((1,), (0,)))
        parts = product.reshape(4, part, size)
        parts = lax.all_to_all(parts, "row", 0, 0, axis_index_groups=X_GROUPS)
        inner = mine + COEF_C * jnp.sum(parts, 0)
        inner = lax.all_gather(inner, "row", axis=0, tiled=True, axis_index_groups=X_GROUPS)
    with jax.named_scope("second_product"):
        packed = local(
            tail_kernel,
            [PACKED] * 8,
            [core, q],
            dot(gram_kept, inner, ((1,), (1,))),
            dot(gram_given, inner, ((1,), (1,))),
        )
        sums = []
        for blocks in (packed[:4], packed[4:]):
            blocks = [b_shift(block, s) if s else block for s, block in enumerate(blocks)]
            sums.append(blocks[0] + blocks[1] + blocks[2] + blocks[3])
    with jax.named_scope("swap_back"):
        other = swap_q(sums[0])
        return local(final_kernel, [iterate.shape], [q], iterate, sums[1], other)[0]


def solution(mesh):
    placed = (P("row", "col"),)
    return jax.shard_map(
        body, mesh=mesh, in_specs=placed, out_specs=P("row", "col"), check_vma=False
    )
```

```python
import math

import jax
import jax.numpy as jnp
from jax import lax
from jax.experimental import pallas as pl
from jax.experimental.pallas import tpu as pltpu
from jax.sharding import PartitionSpec as P

M = 3584
N = 9216

PREC = lax.Precision.HIGHEST
COEF_A = 3.4445
COEF_B = -4.775
COEF_C = 2.0315
AXES = ("row", "col")

X_GROUPS = [[zl * 4 + x for x in range(4)] for zl in range(8)]
B_GROUPS = [[(q * 4 + b) * 4 + x for b in range(4)] for q in range(2) for x in range(4)]
Y_GROUPS = [[y * 4 + k for y in range(4)] for k in range(4)]


def device(x, y, z, core):
    return ((z % 8) * 4 + x) * 16 + y * 4 + (z // 8) * 2 + core


CHIPS = [(x, y, z) for x in range(4) for y in range(4) for z in range(16)]
A_GROUPS = [
    [device(x, y, (a * 4 + b), c) for a in range(4)]
    for x in range(4) for y in range(4) for b in range(4) for c in range(2)
]


def permute(value, target):
    pairs = [
        (device(x, y, z, c), device(*target(x, y, z, c))) for x, y, z in CHIPS for c in range(2)
    ]
    return lax.ppermute(value, AXES, pairs)


def swap_q(value):
    return permute(value, lambda x, y, z, c: (x, y, z ^ 4, c))


def swap_core(value):
    return permute(value, lambda x, y, z, c: (x, y, z, 1 - c))


def b_shift(value, step):
    return permute(value, lambda x, y, z, c: (x, y, z // 4 * 4 + (z + step) % 4, c))


def dot(left, right, dims):
    return lax.dot_general(
        left, right, (dims, ((), ())), precision=PREC, preferred_element_type=jnp.float32
    )


def local(kernel, shapes, index, *arrays, scratch=()):
    vmem = pl.BlockSpec(memory_space=pltpu.VMEM)
    return pl.pallas_call(
        kernel,
        out_shape=[jax.ShapeDtypeStruct(shape, jnp.float32) for shape in shapes],
        in_specs=[pl.BlockSpec(memory_space=pltpu.SMEM)] + [vmem] * len(arrays),
        out_specs=[vmem] * len(shapes),
        scratch_shapes=[pltpu.VMEM(shape, jnp.float32) for shape in scratch],
        compiler_params=pltpu.CompilerParams(vmem_limit_bytes=16 * 2**20),
    )(jnp.stack(index).astype(jnp.int32), *arrays)


ROWS, DEPTH = 112, 288
PACKED = (256, 128)


def pack(packed, value):
    packed[0:ROWS, :] = value[:, 0:128]
    packed[ROWS : 2 * ROWS, :] = value[:, 128:256]
    packed[240:256, :] = jnp.zeros((16, 128), jnp.float32)
    for g in range(4):
        n = min(32, ROWS - 32 * g)
        packed[224 : 224 + n, 32 * g : 32 * g + 32] = value[32 * g : 32 * g + n, 256:DEPTH]


def unpack(value, packed, at):
    value[0:ROWS, at : at + 128] = packed[0:ROWS, :]
    value[0:ROWS, at + 128 : at + 256] = packed[ROWS : 2 * ROWS, :]
    for g in range(4):
        n = min(32, ROWS - 32 * g)
        value[32 * g : 32 * g + n, at + 256 : at + DEPTH] = packed[
            224 : 224 + n, 32 * g : 32 * g + 32
        ]


def send_kernel(index, iterate, sent, own):
    for q in range(2):

        @pl.when(index[0] == q)
        def _():
            pack(sent, iterate[:, DEPTH * (1 - q) : DEPTH * (2 - q)])
            own[...] = iterate[:, DEPTH * q : DEPTH * (q + 1)]


def block_kernel(index, own, other, block, blocks, wide):
    part = DEPTH // 4

    def place(q):
        flipped = wide[...].T
        for k in range(4):
            at = k * 2 * ROWS + q * ROWS
            value = flipped[k * part : (k + 1) * part, 0:ROWS]
            block[:, at : at + ROWS] = value

    for q in range(2):

        @pl.when(index[0] == q)
        def _():
            wide[0:ROWS, 0:DEPTH] = own[...]
            place(q)
            unpack(wide, other, 0)
            place(1 - q)

    for n in range(4):
        blocks[n, :, :] = block[...]


def faces_kernel(index, from_x, from_b, right, kept, given, mine):
    b, core, x = index[0], index[1], index[2]
    part, wide = DEPTH // 4, 2 * ROWS
    for n in range(4):
        for k in range(4):
            rows, lanes = pl.ds(k * part, part), pl.ds(k * wide, wide)
            right[rows, n * wide : (n + 1) * wide] = from_x[n, :, lanes]
            face = (kept, given)[n // 2]
            source = lax.rem(b + 2 * core + n, 4)
            face[rows, n % 2 * wide : (n % 2 + 1) * wide] = from_b[source, :, lanes]
    mine[...] = COEF_B * right[pl.ds(pl.multiple_of(x * part, 8), part), :]


def split(value):
    first = value.astype(jnp.bfloat16)
    value = value - first.astype(jnp.float32)
    second = value.astype(jnp.bfloat16)
    value = value - second.astype(jnp.float32)
    return first, second, value.astype(jnp.bfloat16)


def gram_kernel(index, left, right, product):
    deep, dims = 256, (((0,), (0,)), ((), ()))
    one = split(left[deep:DEPTH, :])
    two = split(right[deep:DEPTH, :])
    pairs = ((0, 0), (0, 1), (1, 0), (1, 1), (0, 2), (2, 0))
    rest = lax.dot_general(
        jnp.concatenate([one[i] for i, _ in pairs], 0),
        jnp.concatenate([two[j] for _, j in pairs], 0),
        dims,
        preferred_element_type=jnp.float32,
    )
    product[...] = rest + dot(left[0:deep, :], right[0:deep, :], dims[0])


def tail_kernel(index, kept, given, *refs):
    core, q = index[0], index[1]
    packed, kept_rows, given_rows = refs[:8], refs[8], refs[9]
    kept_rows[...] = kept[...].T
    given_rows[...] = given[...].T
    for c in range(2):

        @pl.when(core == c)
        def _():
            for s in range(4):
                source = (kept_rows, given_rows)[(s // 2 + c) % 2]
                for n, part in enumerate((1 - q, q)):
                    at = pl.multiple_of(s % 2 * 2 * ROWS + part * ROWS, 8)
                    pack(packed[4 * n + s], source[pl.ds(at, ROWS), :])


def final_kernel(index, iterate, own, other, update):
    scale = 0.2 * math.sqrt(max(M, N))

    def put(rows, lanes, applied):
        update[rows, lanes] = (COEF_A * iterate[rows, lanes] + applied) * scale

    for q in range(2):

        @pl.when(index[0] == q)
        def _():
            for packed, at in ((own, DEPTH * q), (other, DEPTH * (1 - q))):
                put(slice(0, ROWS), slice(at, at + 128), packed[0:ROWS, :])
                put(slice(0, ROWS), slice(at + 128, at + 256), packed[ROWS : 2 * ROWS, :])
                for g in range(4):
                    n = min(32, ROWS - 32 * g)
                    rest = packed[224 : 224 + n, 32 * g : 32 * g + 32]
                    put(slice(32 * g, 32 * g + n), slice(at + 256, at + DEPTH), rest)


def tiles(value):
    rows, lanes = value.shape
    value = value.reshape(rows // 8, 8, lanes // 128, 128).transpose(0, 2, 1, 3)
    value = value.reshape(-1, 8, 128)
    each = -(-value.shape[0] // 4)
    value = jnp.pad(value, ((0, 4 * each - value.shape[0]), (0, 0), (0, 0)))
    return value.reshape(4, each, 8, 128)


def from_tiles(pieces, shape):
    rows, lanes = shape
    value = pieces.reshape(-1, 8, 128)[: rows // 8 * (lanes // 128)]
    value = value.reshape(rows // 8, lanes // 128, 8, 128).transpose(0, 2, 1, 3)
    return value.reshape(rows, lanes)


def body(iterate):
    part, size = DEPTH // 4, 8 * ROWS
    half, chunk = size // 2, size // 8
    row, col = lax.axis_index("row"), lax.axis_index("col")
    core = col % 2
    a = col // 2 % 2 * 2 + row // 16
    x, b, q = row % 4, row // 4 % 4, row // 16

    with jax.named_scope("swap_columns"):
        sent, own = local(send_kernel, [PACKED, (ROWS, DEPTH)], [q], iterate)
        other = swap_q(sent)
    with jax.named_scope("faces"):
        block, blocks = local(
            block_kernel, [(part, size), (4, part, size)], [q], own, other, scratch=[(128, 384)]
        )
        from_x = lax.all_to_all(blocks, "row", 0, 0, axis_index_groups=X_GROUPS)
        from_b = lax.all_gather(block, "row", axis=0, axis_index_groups=B_GROUPS)
        right, kept, given, mine = local(
            faces_kernel,
            [(DEPTH, size), (DEPTH, half), (DEPTH, half), (part, size)],
            [b, core, x],
            from_x,
            from_b,
        )

    with jax.named_scope("gram"):
        (partial,) = local(gram_kernel, [(half, size)], [core], given, right)
        partial = swap_core(partial)
        (total,) = local(gram_kernel, [(half, size)], [core], kept, right)
        total = total + partial
    with jax.named_scope("reduce_y"):
        parts = lax.all_to_all(
            total.reshape(4, chunk, size), "col", 0, 0, axis_index_groups=Y_GROUPS
        )
        near = jnp.sum(parts, 0)
    with jax.named_scope("reduce_a"):
        pieces = tiles(near)
        piece = lax.dynamic_index_in_dim(pieces, a, 0, False)
        for step in (2, 1, 3):
            sent = lax.dynamic_index_in_dim(pieces, (a + step) % 4, 0, False)
            piece = piece + permute(sent, lambda x, y, z, c: (x, y, (z + 4 * step) % 16, c))
    with jax.named_scope("gather_a"):
        pieces = lax.all_gather(piece, AXES, axis=0, axis_index_groups=A_GROUPS)
        near = from_tiles(pieces, near.shape)
    with jax.named_scope("gather_y"):
        parts = jnp.broadcast_to(near, (4,) + near.shape)
        parts = lax.all_to_all(parts, "col", 0, 0, axis_index_groups=Y_GROUPS)
        gram_kept = parts.reshape(half, size)
    with jax.named_scope("gather_core"):
        gram_given = swap_core(gram_kept)

    with jax.named_scope("first_product"):
        product = lax.optimization_barrier(dot(kept, gram_kept, ((1,), (0,))))
        product = product + dot(given, gram_given, ((1,), (0,)))
        parts = product.reshape(4, part, size)
        parts = lax.all_to_all(parts, "row", 0, 0, axis_index_groups=X_GROUPS)
        inner = mine + COEF_C * jnp.sum(parts, 0)
        inner = lax.all_gather(inner, "row", axis=0, tiled=True, axis_index_groups=X_GROUPS)
    with jax.named_scope("second_product"):
        packed = local(
            tail_kernel,
            [PACKED] * 8,
            [core, q],
            dot(inner, gram_kept, ((1,), (1,))),
            dot(inner, gram_given, ((1,), (1,))),
            scratch=[(half, DEPTH)] * 2,
        )
        sums = []
        for blocks in (packed[:4], packed[4:]):
            blocks = [b_shift(block, s) if s else block for s, block in enumerate(blocks)]
            sums.append(blocks[0] + blocks[1] + blocks[2] + blocks[3])
    with jax.named_scope("swap_back"):
        other = swap_q(sums[0])
        return local(final_kernel, [iterate.shape], [q], iterate, sums[1], other)[0]


def solution(mesh):
    placed = (P("row", "col"),)
    return jax.shard_map(
        body, mesh=mesh, in_specs=placed, out_specs=P("row", "col"), check_vma=False
    )
```

```python
import math

import jax
import jax.numpy as jnp
from jax import lax
from jax.experimental import pallas as pl
from jax.experimental.pallas import tpu as pltpu
from jax.sharding import PartitionSpec as P

M = 3584
N = 9216

PREC = lax.Precision.HIGHEST
COEF_A = 3.4445
COEF_B = -4.775
COEF_C = 2.0315
AXES = ("row", "col")

X_GROUPS = [[zl * 4 + x for x in range(4)] for zl in range(8)]
B_GROUPS = [[(q * 4 + b) * 4 + x for b in range(4)] for q in range(2) for x in range(4)]
Y_GROUPS = [[y * 4 + k for y in range(4)] for k in range(4)]


def device(x, y, z, core):
    return ((z % 8) * 4 + x) * 16 + y * 4 + (z // 8) * 2 + core


CHIPS = [(x, y, z) for x in range(4) for y in range(4) for z in range(16)]
A_GROUPS = [
    [device(x, y, (a * 4 + b), c) for a in range(4)]
    for x in range(4) for y in range(4) for b in range(4) for c in range(2)
]


def permute(value, target):
    pairs = [
        (device(x, y, z, c), device(*target(x, y, z, c))) for x, y, z in CHIPS for c in range(2)
    ]
    return lax.ppermute(value, AXES, pairs)


def swap_q(value):
    return permute(value, lambda x, y, z, c: (x, y, z ^ 4, c))


def swap_core(value):
    return permute(value, lambda x, y, z, c: (x, y, z, 1 - c))


def b_shift(value, step):
    return permute(value, lambda x, y, z, c: (x, y, z // 4 * 4 + (z + step) % 4, c))


def dot(left, right, dims):
    return lax.dot_general(
        left, right, (dims, ((), ())), precision=PREC, preferred_element_type=jnp.float32
    )


def local(kernel, shapes, index, *arrays, scratch=()):
    vmem = pl.BlockSpec(memory_space=pltpu.VMEM)
    return pl.pallas_call(
        kernel,
        out_shape=[jax.ShapeDtypeStruct(shape, jnp.float32) for shape in shapes],
        in_specs=[pl.BlockSpec(memory_space=pltpu.SMEM)] + [vmem] * len(arrays),
        out_specs=[vmem] * len(shapes),
        scratch_shapes=[pltpu.VMEM(shape, jnp.float32) for shape in scratch],
        compiler_params=pltpu.CompilerParams(vmem_limit_bytes=16 * 2**20),
    )(jnp.stack(index).astype(jnp.int32), *arrays)


ROWS, DEPTH = 112, 288
PACKED = (256, 128)


def pack(packed, value):
    packed[0:ROWS, :] = value[:, 0:128]
    packed[ROWS : 2 * ROWS, :] = value[:, 128:256]
    packed[240:256, :] = jnp.zeros((16, 128), jnp.float32)
    for g in range(4):
        n = min(32, ROWS - 32 * g)
        packed[224 : 224 + n, 32 * g : 32 * g + 32] = value[32 * g : 32 * g + n, 256:DEPTH]


def unpack(value, packed, at):
    value[0:ROWS, at : at + 128] = packed[0:ROWS, :]
    value[0:ROWS, at + 128 : at + 256] = packed[ROWS : 2 * ROWS, :]
    for g in range(4):
        n = min(32, ROWS - 32 * g)
        value[32 * g : 32 * g + n, at + 256 : at + DEPTH] = packed[
            224 : 224 + n, 32 * g : 32 * g + 32
        ]


def send_kernel(index, iterate, sent, own):
    for q in range(2):

        @pl.when(index[0] == q)
        def _():
            pack(sent, iterate[:, DEPTH * (1 - q) : DEPTH * (2 - q)])
            own[...] = iterate[:, DEPTH * q : DEPTH * (q + 1)]


def place(block, wide, q):
    part = DEPTH // 4
    flipped = wide[...].T
    for k in range(4):
        at = k * 2 * ROWS + q * ROWS
        block[:, at : at + ROWS] = flipped[k * part : (k + 1) * part, 0:ROWS]


def own_kernel(index, own, block, wide):
    wide[0:ROWS, 0:DEPTH] = own[...]
    block[...] = jnp.zeros(block.shape, jnp.float32)
    for q in range(2):

        @pl.when(index[0] == q)
        def _():
            place(block, wide, q)


def block_kernel(index, own, other, block, blocks, wide):
    block[...] = own[...]
    unpack(wide, other, 0)
    for q in range(2):

        @pl.when(index[0] == q)
        def _():
            place(block, wide, 1 - q)

    for n in range(4):
        blocks[n, :, :] = block[...]


def faces_kernel(index, from_x, from_b, right, kept, given, mine):
    b, core, x = index[0], index[1], index[2]
    part, wide = DEPTH // 4, 2 * ROWS
    for n in range(4):
        for k in range(4):
            rows, lanes = pl.ds(k * part, part), pl.ds(k * wide, wide)
            right[rows, n * wide : (n + 1) * wide] = from_x[n, :, lanes]
            face = (kept, given)[n // 2]
            source = lax.rem(b + 2 * core + n, 4)
            face[rows, n % 2 * wide : (n % 2 + 1) * wide] = from_b[source, :, lanes]
    mine[...] = COEF_B * right[pl.ds(pl.multiple_of(x * part, 8), part), :]


def split(value):
    first = value.astype(jnp.bfloat16)
    value = value - first.astype(jnp.float32)
    second = value.astype(jnp.bfloat16)
    value = value - second.astype(jnp.float32)
    return first, second, value.astype(jnp.bfloat16)


def gram_kernel(index, left, right, product):
    deep, dims = 256, (((0,), (0,)), ((), ()))
    one = split(left[deep:DEPTH, :])
    two = split(right[deep:DEPTH, :])
    pairs = ((0, 0), (0, 1), (1, 0), (1, 1), (0, 2), (2, 0))
    rest = lax.dot_general(
        jnp.concatenate([one[i] for i, _ in pairs], 0),
        jnp.concatenate([two[j] for _, j in pairs], 0),
        dims,
        preferred_element_type=jnp.float32,
    )
    product[...] = rest + dot(left[0:deep, :], right[0:deep, :], dims[0])


def tail_kernel(index, kept, given, *refs):
    core, q = index[0], index[1]
    packed, kept_rows, given_rows = refs[:8], refs[8], refs[9]
    kept_rows[...] = kept[...].T
    given_rows[...] = given[...].T
    for c in range(2):

        @pl.when(core == c)
        def _():
            for s in range(4):
                source = (kept_rows, given_rows)[(s // 2 + c) % 2]
                for n, part in enumerate((1 - q, q)):
                    at = pl.multiple_of(s % 2 * 2 * ROWS + part * ROWS, 8)
                    pack(packed[4 * n + s], source[pl.ds(at, ROWS), :])


def final_kernel(index, iterate, own, other, update):
    scale = 0.2 * math.sqrt(max(M, N))

    def put(rows, lanes, applied):
        update[rows, lanes] = (COEF_A * iterate[rows, lanes] + applied) * scale

    for q in range(2):

        @pl.when(index[0] == q)
        def _():
            for packed, at in ((own, DEPTH * q), (other, DEPTH * (1 - q))):
                put(slice(0, ROWS), slice(at, at + 128), packed[0:ROWS, :])
                put(slice(0, ROWS), slice(at + 128, at + 256), packed[ROWS : 2 * ROWS, :])
                for g in range(4):
                    n = min(32, ROWS - 32 * g)
                    rest = packed[224 : 224 + n, 32 * g : 32 * g + 32]
                    put(slice(32 * g, 32 * g + n), slice(at + 256, at + DEPTH), rest)


def tiles(value):
    rows, lanes = value.shape
    value = value.reshape(rows // 8, 8, lanes // 128, 128).transpose(0, 2, 1, 3)
    value = value.reshape(-1, 8, 128)
    each = -(-value.shape[0] // 4)
    value = jnp.pad(value, ((0, 4 * each - value.shape[0]), (0, 0), (0, 0)))
    return value.reshape(4, each, 8, 128)


def from_tiles(pieces, shape):
    rows, lanes = shape
    value = pieces.reshape(-1, 8, 128)[: rows // 8 * (lanes // 128)]
    value = value.reshape(rows // 8, lanes // 128, 8, 128).transpose(0, 2, 1, 3)
    return value.reshape(rows, lanes)


def body(iterate):
    part, size = DEPTH // 4, 8 * ROWS
    half, chunk = size // 2, size // 8
    row, col = lax.axis_index("row"), lax.axis_index("col")
    core = col % 2
    a = col // 2 % 2 * 2 + row // 16
    x, b, q = row % 4, row // 4 % 4, row // 16

    with jax.named_scope("swap_columns"):
        sent, own = local(send_kernel, [PACKED, (ROWS, DEPTH)], [q], iterate)
        other = swap_q(sent)
        (own,) = local(own_kernel, [(part, size)], [q], own, scratch=[(128, 384)])
    with jax.named_scope("faces"):
        block, blocks = local(
            block_kernel, [(part, size), (4, part, size)], [q], own, other, scratch=[(128, 384)]
        )
        from_x = lax.all_to_all(blocks, "row", 0, 0, axis_index_groups=X_GROUPS)
        from_b = lax.all_gather(block, "row", axis=0, axis_index_groups=B_GROUPS)
        right, kept, given, mine = local(
            faces_kernel,
            [(DEPTH, size), (DEPTH, half), (DEPTH, half), (part, size)],
            [b, core, x],
            from_x,
            from_b,
        )

    with jax.named_scope("gram"):
        (partial,) = local(gram_kernel, [(half, size)], [core], given, right)
        partial = swap_core(partial)
        (total,) = local(gram_kernel, [(half, size)], [core], kept, right)
        total = total + partial
    with jax.named_scope("reduce_y"):
        parts = lax.all_to_all(
            total.reshape(4, chunk, size), "col", 0, 0, axis_index_groups=Y_GROUPS
        )
        near = jnp.sum(parts, 0)
    with jax.named_scope("reduce_a"):
        pieces = tiles(near)
        piece = lax.dynamic_index_in_dim(pieces, a, 0, False)
        for step in (2, 3, 1):
            sent = lax.dynamic_index_in_dim(pieces, (a + step) % 4, 0, False)
            piece = piece + permute(sent, lambda x, y, z, c: (x, y, (z + 4 * step) % 16, c))
    with jax.named_scope("gather_a"):
        pieces = lax.all_gather(piece, AXES, axis=0, axis_index_groups=A_GROUPS)
        near = from_tiles(pieces, near.shape)
    with jax.named_scope("gather_y"):
        parts = jnp.broadcast_to(near, (4,) + near.shape)
        parts = lax.all_to_all(parts, "col", 0, 0, axis_index_groups=Y_GROUPS)
        gram_kept = parts.reshape(half, size)
    with jax.named_scope("gather_core"):
        gram_given = swap_core(gram_kept)

    with jax.named_scope("first_product"):
        product = lax.optimization_barrier(dot(kept, gram_kept, ((1,), (0,))))
        product = product + dot(given, gram_given, ((1,), (0,)))
        parts = product.reshape(4, part, size)
        parts = lax.all_to_all(parts, "row", 0, 0, axis_index_groups=X_GROUPS)
        inner = mine + COEF_C * jnp.sum(parts, 0)
        inner = lax.all_gather(inner, "row", axis=0, tiled=True, axis_index_groups=X_GROUPS)
    with jax.named_scope("second_product"):
        packed = local(
            tail_kernel,
            [PACKED] * 8,
            [core, q],
            dot(inner, gram_kept, ((1,), (1,))),
            dot(inner, gram_given, ((1,), (1,))),
            scratch=[(half, DEPTH)] * 2,
        )
        sums = []
        for blocks in (packed[:4], packed[4:]):
            blocks = [b_shift(block, s) if s else block for s, block in enumerate(blocks)]
            sums.append(blocks[0] + blocks[1] + blocks[2] + blocks[3])
    with jax.named_scope("swap_back"):
        other = swap_q(sums[0])
        return local(final_kernel, [iterate.shape], [q], iterate, sums[1], other)[0]


def solution(mesh):
    placed = (P("row", "col"),)
    return jax.shard_map(
        body, mesh=mesh, in_specs=placed, out_specs=P("row", "col"), check_vma=False
    )
```

```python
import math

import jax
import jax.numpy as jnp
from jax import lax
from jax.experimental import pallas as pl
from jax.experimental.pallas import tpu as pltpu
from jax.sharding import PartitionSpec as P

M = 3584
N = 9216

PREC = lax.Precision.HIGHEST
COEF_A = 3.4445
COEF_B = -4.775
COEF_C = 2.0315
AXES = ("row", "col")

X_GROUPS = [[zl * 4 + x for x in range(4)] for zl in range(8)]
B_GROUPS = [[(q * 4 + b) * 4 + x for b in range(4)] for q in range(2) for x in range(4)]
Y_GROUPS = [[y * 4 + k for y in range(4)] for k in range(4)]


def device(x, y, z, core):
    return ((z % 8) * 4 + x) * 16 + y * 4 + (z // 8) * 2 + core


CHIPS = [(x, y, z) for x in range(4) for y in range(4) for z in range(16)]
A_GROUPS = [
    [device(x, y, (a * 4 + b), c) for a in range(4)]
    for x in range(4) for y in range(4) for b in range(4) for c in range(2)
]


def permute(value, target):
    pairs = [
        (device(x, y, z, c), device(*target(x, y, z, c))) for x, y, z in CHIPS for c in range(2)
    ]
    return lax.ppermute(value, AXES, pairs)


def swap_q(value):
    return permute(value, lambda x, y, z, c: (x, y, z ^ 4, c))


def swap_core(value):
    return permute(value, lambda x, y, z, c: (x, y, z, 1 - c))


def b_shift(value, step):
    return permute(value, lambda x, y, z, c: (x, y, z ^ step, c))


def dot(left, right, dims):
    return lax.dot_general(
        left, right, (dims, ((), ())), precision=PREC, preferred_element_type=jnp.float32
    )


def local(kernel, shapes, index, *arrays, scratch=()):
    vmem = pl.BlockSpec(memory_space=pltpu.VMEM)
    return pl.pallas_call(
        kernel,
        out_shape=[jax.ShapeDtypeStruct(shape, jnp.float32) for shape in shapes],
        in_specs=[pl.BlockSpec(memory_space=pltpu.SMEM)] + [vmem] * len(arrays),
        out_specs=[vmem] * len(shapes),
        scratch_shapes=[pltpu.VMEM(shape, jnp.float32) for shape in scratch],
        compiler_params=pltpu.CompilerParams(vmem_limit_bytes=16 * 2**20),
    )(jnp.stack(index).astype(jnp.int32), *arrays)


ROWS, DEPTH = 112, 288
PACKED = (256, 128)


def pack(packed, value):
    packed[0:ROWS, :] = value[:, 0:128]
    packed[ROWS : 2 * ROWS, :] = value[:, 128:256]
    packed[240:256, :] = jnp.zeros((16, 128), jnp.float32)
    for g in range(4):
        n = min(32, ROWS - 32 * g)
        packed[224 : 224 + n, 32 * g : 32 * g + 32] = value[32 * g : 32 * g + n, 256:DEPTH]


def unpack(value, packed, at):
    value[0:ROWS, at : at + 128] = packed[0:ROWS, :]
    value[0:ROWS, at + 128 : at + 256] = packed[ROWS : 2 * ROWS, :]
    for g in range(4):
        n = min(32, ROWS - 32 * g)
        value[32 * g : 32 * g + n, at + 256 : at + DEPTH] = packed[
            224 : 224 + n, 32 * g : 32 * g + 32
        ]


def send_kernel(index, iterate, sent, own):
    for q in range(2):

        @pl.when(index[0] == q)
        def _():
            pack(sent, iterate[:, DEPTH * (1 - q) : DEPTH * (2 - q)])
            own[...] = iterate[:, DEPTH * q : DEPTH * (q + 1)]


def block_kernel(index, own, other, block, blocks, wide):
    part = DEPTH // 4

    def place(q):
        flipped = wide[...].T
        for k in range(4):
            at = k * 2 * ROWS + q * ROWS
            value = flipped[k * part : (k + 1) * part, 0:ROWS]
            block[:, at : at + ROWS] = value

    for q in range(2):

        @pl.when(index[0] == q)
        def _():
            wide[0:ROWS, 0:DEPTH] = own[...]
            place(q)
            unpack(wide, other, 0)
            place(1 - q)

    for n in range(4):
        blocks[n, :, :] = block[...]


def faces_kernel(index, from_x, from_b, right, kept, given, mine):
    b, core, x = index[0], index[1], index[2]
    part, wide = DEPTH // 4, 2 * ROWS
    for n in range(4):
        for k in range(4):
            rows, lanes = pl.ds(k * part, part), pl.ds(k * wide, wide)
            right[rows, n * wide : (n + 1) * wide] = from_x[n, :, lanes]
            face = (kept, given)[n // 2]
            source = lax.bitwise_xor(b, lax.rem(2 * core + n, 4))
            face[rows, n % 2 * wide : (n % 2 + 1) * wide] = from_b[source, :, lanes]
    mine[...] = COEF_B * right[pl.ds(pl.multiple_of(x * part, 8), part), :]


def split(value):
    first = value.astype(jnp.bfloat16)
    value = value - first.astype(jnp.float32)
    second = value.astype(jnp.bfloat16)
    value = value - second.astype(jnp.float32)
    return first, second, value.astype(jnp.bfloat16)


def gram_kernel(index, left, right, product):
    deep, dims = 256, (((0,), (0,)), ((), ()))
    one = split(left[deep:DEPTH, :])
    two = split(right[deep:DEPTH, :])
    pairs = ((0, 0), (0, 1), (1, 0), (1, 1), (0, 2), (2, 0))
    rest = lax.dot_general(
        jnp.concatenate([one[i] for i, _ in pairs], 0),
        jnp.concatenate([two[j] for _, j in pairs], 0),
        dims,
        preferred_element_type=jnp.float32,
    )
    product[...] = rest + dot(left[0:deep, :], right[0:deep, :], dims[0])


def tail_kernel(index, kept, given, *refs):
    core, q = index[0], index[1]
    packed, kept_rows, given_rows = refs[:8], refs[8], refs[9]
    kept_rows[...] = kept[...].T
    given_rows[...] = given[...].T
    for c in range(2):

        @pl.when(core == c)
        def _():
            for s in range(4):
                source = (kept_rows, given_rows)[(s // 2 + c) % 2]
                for n, part in enumerate((1 - q, q)):
                    at = pl.multiple_of(s % 2 * 2 * ROWS + part * ROWS, 8)
                    pack(packed[4 * n + s], source[pl.ds(at, ROWS), :])


def final_kernel(index, iterate, own, other, update):
    scale = 0.2 * math.sqrt(max(M, N))

    def put(rows, lanes, applied):
        update[rows, lanes] = (COEF_A * iterate[rows, lanes] + applied) * scale

    for q in range(2):

        @pl.when(index[0] == q)
        def _():
            for packed, at in ((own, DEPTH * q), (other, DEPTH * (1 - q))):
                put(slice(0, ROWS), slice(at, at + 128), packed[0:ROWS, :])
                put(slice(0, ROWS), slice(at + 128, at + 256), packed[ROWS : 2 * ROWS, :])
                for g in range(4):
                    n = min(32, ROWS - 32 * g)
                    rest = packed[224 : 224 + n, 32 * g : 32 * g + 32]
                    put(slice(32 * g, 32 * g + n), slice(at + 256, at + DEPTH), rest)


def tiles(value):
    rows, lanes = value.shape
    value = value.reshape(rows // 8, 8, lanes // 128, 128).transpose(0, 2, 1, 3)
    value = value.reshape(-1, 8, 128)
    each = -(-value.shape[0] // 4)
    value = jnp.pad(value, ((0, 4 * each - value.shape[0]), (0, 0), (0, 0)))
    return value.reshape(4, each, 8, 128)


def from_tiles(pieces, shape):
    rows, lanes = shape
    value = pieces.reshape(-1, 8, 128)[: rows // 8 * (lanes // 128)]
    value = value.reshape(rows // 8, lanes // 128, 8, 128).transpose(0, 2, 1, 3)
    return value.reshape(rows, lanes)


def body(iterate):
    part, size = DEPTH // 4, 8 * ROWS
    half, chunk = size // 2, size // 8
    row, col = lax.axis_index("row"), lax.axis_index("col")
    core = col % 2
    a = col // 2 % 2 * 2 + row // 16
    x, b, q = row % 4, row // 4 % 4, row // 16

    with jax.named_scope("swap_columns"):
        sent, own = local(send_kernel, [PACKED, (ROWS, DEPTH)], [q], iterate)
        other = swap_q(sent)
    with jax.named_scope("faces"):
        block, blocks = local(
            block_kernel, [(part, size), (4, part, size)], [q], own, other, scratch=[(128, 384)]
        )
        from_x = lax.all_to_all(blocks, "row", 0, 0, axis_index_groups=X_GROUPS)
        from_b = lax.all_gather(block, "row", axis=0, axis_index_groups=B_GROUPS)
        right, kept, given, mine = local(
            faces_kernel,
            [(DEPTH, size), (DEPTH, half), (DEPTH, half), (part, size)],
            [b, core, x],
            from_x,
            from_b,
        )

    with jax.named_scope("gram"):
        (partial,) = local(gram_kernel, [(half, size)], [core], given, right)
        partial = swap_core(partial)
        (total,) = local(gram_kernel, [(half, size)], [core], kept, right)
        total = total + partial
    with jax.named_scope("reduce_y"):
        parts = lax.all_to_all(
            total.reshape(4, chunk, size), "col", 0, 0, axis_index_groups=Y_GROUPS
        )
        near = jnp.sum(parts, 0)
    with jax.named_scope("reduce_a"):
        pieces = tiles(near)
        piece = lax.dynamic_index_in_dim(pieces, a, 0, False)
        for step in (2, 1, 3):
            sent = lax.dynamic_index_in_dim(pieces, (a + step) % 4, 0, False)
            piece = piece + permute(sent, lambda x, y, z, c: (x, y, (z + 4 * step) % 16, c))
    with jax.named_scope("gather_a"):
        pieces = lax.all_gather(piece, AXES, axis=0, axis_index_groups=A_GROUPS)
        near = from_tiles(pieces, near.shape)
    with jax.named_scope("gather_y"):
        parts = jnp.broadcast_to(near, (4,) + near.shape)
        parts = lax.all_to_all(parts, "col", 0, 0, axis_index_groups=Y_GROUPS)
        gram_kept = parts.reshape(half, size)
    with jax.named_scope("gather_core"):
        gram_given = swap_core(gram_kept)

    with jax.named_scope("first_product"):
        product = lax.optimization_barrier(dot(kept, gram_kept, ((1,), (0,))))
        product = product + dot(given, gram_given, ((1,), (0,)))
        parts = product.reshape(4, part, size)
        parts = lax.all_to_all(parts, "row", 0, 0, axis_index_groups=X_GROUPS)
        inner = mine + COEF_C * jnp.sum(parts, 0)
        inner = lax.all_gather(inner, "row", axis=0, tiled=True, axis_index_groups=X_GROUPS)
    with jax.named_scope("second_product"):
        packed = local(
            tail_kernel,
            [PACKED] * 8,
            [core, q],
            dot(inner, gram_kept, ((1,), (1,))),
            dot(inner, gram_given, ((1,), (1,))),
            scratch=[(half, DEPTH)] * 2,
        )
        sums = []
        for blocks in (packed[:4], packed[4:]):
            blocks = [b_shift(block, s) if s else block for s, block in enumerate(blocks)]
            sums.append(blocks[0] + blocks[1] + blocks[2] + blocks[3])
    with jax.named_scope("swap_back"):
        other = swap_q(sums[0])
        return local(final_kernel, [iterate.shape], [q], iterate, sums[1], other)[0]


def solution(mesh):
    placed = (P("row", "col"),)
    return jax.shard_map(
        body, mesh=mesh, in_specs=placed, out_specs=P("row", "col"), check_vma=False
    )
```
